128 devices in a mesh: blk: 16 (over z, y_lo, core), quad: 8 (over y_hi, x).
Axes of the slice: x: 4, y: 4 (y_hi: 2, y_lo: 2; y = y_hi * 2 + y_lo), z: 4, core: 2. Of those that a mesh axis runs over, the one named last changes fastest.
Arguments:
- positions: bfloat16 [3, 65536], P(None, ('blk', 'quad')), may hold values from -1 to 1
- normals: bfloat16 [3, 65536], P(None, ('blk', 'quad')), may hold values from -1 to 1, as said below
- patch_area: bfloat16 [65536], P(('blk', 'quad')), may hold values from 0.00048828125 to 0.00390625
- reflect: float32 [65536], P(('blk', 'quad')), may hold values from 0.3 to 0.9
- emission: float32 [65536, 128], P(('blk', 'quad')), may hold values from 0.1 to 1
- radiosity: float32 [65536, 128], P(('blk', 'quad')), may hold values from 0.2 to 2
- visible: int32 [512, 512], P('blk'), may hold values from 0 to 1, as said below
Outputs:
- updated: float32 [65536, 128], P(('blk', 'quad'))
The draws below stay inside these ranges and needn't reach their ends.
Inputs may be any that keep to these rules, and one draw needn't show every extreme that they name: Each column of normals has unit length up to rounding to bfloat16. visible[a, b] equals visible[b, a].
All inputs are finite; a program needn't handle non-finite values.
Results may differ from the reference program's by a relative error of at most 0.0003.
Values may be sent and summed in bfloat16 or wider, within the bound.
No kernel may reach another device: no remote copies, remote signals or barrier semaphores. Data moves between devices by JAX's collectives and lax.ppermute only.
A program may use at most 128 MiB of HBM per device.

```python
import math
import jax
import jax.numpy as jnp
from jax import lax

CASES = 128
TILE = 128
BLOCK = 4096
PATCHES = 65536


def draw_normals(key, part):
    key = jax.random.fold_in(key, 5)
    samples = jax.random.normal(key, (3, PATCHES), jnp.float32)
    length = jnp.sqrt(jnp.sum(samples * samples, axis=0, keepdims=True) + 1e-12)
    return (samples / length).astype(jnp.bfloat16)


def draw_visible(key, part):
    key = jax.random.fold_in(key, 11)
    key_density, key_tiles = jax.random.split(key)
    tile_count = PATCHES // TILE
    block_count = PATCHES // BLOCK
    per_block = BLOCK // TILE
    density = jax.random.randint(key_density, (block_count, block_count), 0, 5)
    block_row = jnp.arange(block_count)[:, None]
    block_col = jnp.arange(block_count)[None, :]
    density = jnp.where(block_row <= block_col, density, density.T)
    tile_draw = jax.random.randint(key_tiles, (tile_count, tile_count), 0, 4)
    row_idx = jnp.arange(tile_count)[:, None]
    col_idx = jnp.arange(tile_count)[None, :]
    tile_draw = jnp.where(row_idx <= col_idx, tile_draw, tile_draw.T)
    owner = jnp.arange(tile_count) // per_block
    tile_density = density[owner][:, owner]
    return (tile_draw < tile_density).astype(jnp.int32)


def block_levels(own_key, extent, cuts, low, high):
    def one(position, parts):
        heights = jax.random.uniform(jax.random.fold_in(jax.random.fold_in(own_key, 6), position), (parts,), jnp.float32, low / len(cuts), high / len(cuts))
        return jnp.repeat(jnp.exp(heights), extent[position] // parts).reshape((-1,) + (1,) * (len(extent) - position - 1))

    level = one(*cuts[0])
    for cut in cuts[1:]:
        level = level * one(*cut)
    return level


def setup_inputs(seed: int = 0) -> dict:
    key_of = jax.random.split(jax.random.key(seed), 8)
    positions = jnp.clip(jax.random.uniform(key_of[0], (3, PATCHES), jnp.float32, -1.0, 1.0) * block_levels(key_of[0], (3, PATCHES), ((1, 128),), -0.4, 0.0), -1.0, 1.0).astype(jnp.bfloat16)
    normals = draw_normals(jax.random.fold_in(key_of[7], 71), 0)
    patch_area = jnp.clip(jnp.exp(math.log(0.00390625) - 2.0794415 * jax.random.uniform(key_of[2], (PATCHES,), jnp.float32) ** block_levels(key_of[2], (PATCHES,), ((0, 128),), -0.2, 0.2)), 0.00048828125, 0.00390625).astype(jnp.bfloat16)
    reflect = jnp.clip(0.3 + 0.59999996 * jax.random.uniform(key_of[3], (PATCHES,), jnp.float32) ** block_levels(key_of[3], (PATCHES,), ((0, 128),), -0.2, 0.2), 0.3, 0.9)
    emission = jnp.clip(jnp.exp(math.log(1.0) - 2.3025851 * jax.random.uniform(key_of[4], (PATCHES, CASES), jnp.float32) ** block_levels(key_of[4], (PATCHES, CASES), ((0, 128),), -0.2, 0.2)), 0.1, 1.0)
    radiosity = jnp.clip(jnp.exp(math.log(2.0) - 2.3025851 * jax.random.uniform(key_of[5], (PATCHES, CASES), jnp.float32) ** block_levels(key_of[5], (PATCHES, CASES), ((0, 128),), -0.2, 0.2)), 0.2, 2.0)
    visible = draw_visible(jax.random.fold_in(key_of[7], 71), 0)
    return dict(positions=positions, normals=normals, patch_area=patch_area, reflect=reflect, emission=emission, radiosity=radiosity, visible=visible)


def kernel_tile(row_geometry, col_geometry):
    delta_x = col_geometry[0][None, :] - row_geometry[0][:, None]
    delta_y = col_geometry[1][None, :] - row_geometry[1][:, None]
    delta_z = col_geometry[2][None, :] - row_geometry[2][:, None]
    facing_row = jnp.maximum(row_geometry[3][:, None] * delta_x + row_geometry[4][:, None] * delta_y + row_geometry[5][:, None] * delta_z, 0.0)
    facing_col = jnp.maximum(-(col_geometry[3][None, :] * delta_x + col_geometry[4][None, :] * delta_y + col_geometry[5][None, :] * delta_z), 0.0)
    distance = delta_x * delta_x + delta_y * delta_y + delta_z * delta_z
    denominator = distance + (row_geometry[6][:, None] + col_geometry[6][None, :])
    return facing_row * facing_col / (math.pi * denominator * denominator)


def reference(positions, normals, patch_area, reflect, emission, radiosity, visible):
    geometry = jnp.concatenate([positions.astype(jnp.float32), normals.astype(jnp.float32), patch_area.astype(jnp.float32)[None, :]], 0)
    weighted = (patch_area.astype(jnp.float32)[:, None] * radiosity).astype(jnp.bfloat16)
    band_rows = math.gcd(512, PATCHES)
    band_count = PATCHES // band_rows
    row_geoms = geometry.reshape(7, band_count, band_rows).transpose(1, 0, 2)
    band_masks = visible.reshape(band_count, band_rows // TILE, PATCHES // TILE)

    def row_band(items):
        band_geom, band_mask = items
        kernel = kernel_tile(band_geom, geometry)
        shaped = kernel.reshape(band_rows // TILE, TILE, PATCHES // TILE, TILE) * band_mask[:, None, :, None].astype(jnp.float32)
        coupling = shaped.reshape(band_rows, PATCHES).astype(jnp.bfloat16)
        return jnp.dot(coupling, weighted, preferred_element_type=jnp.float32)

    irradiation = lax.map(row_band, (row_geoms, band_masks)).reshape(PATCHES, CASES)
    return emission + reflect[:, None] * irradiation
```

```python
import functools
import math

import numpy as np

import jax
import jax.numpy as jnp
from jax import lax
from jax.experimental import pallas as pl
from jax.experimental.pallas import tpu as pltpu
from jax.sharding import PartitionSpec as P

BF16, F32 = jnp.bfloat16, jnp.float32
AXES = ("blk", "quad")
SUB = 512
TILE = 128
CASES = 128
TILES = SUB // TILE
GEOM = 16 * TILES
MSG = SUB + GEOM
SLOTS = 64
MASK = 32
CHUNK = 512
ROWS = 1024
VMEM = 56 << 20

SIZE, ALONG, ONES = 8, 11, 14
PARTS = 32


def expansions():
    den, face_row, face_col = (np.zeros((128, SLOTS), np.float32) for _ in range(3))
    for i in range(3):
        den[i, i] = -2
        den[ONES, SIZE + i] = 1
        den[SIZE + i, ONES + i] = 1
        face_row[3 + i, i] = 1
        face_row[ALONG + i, ONES + i] = -1
        face_col[i, 3 + i] = 1
        face_col[ONES, ALONG + i] = -1
    return np.stack([den, face_row, face_col])


def params(**kw):
    return pltpu.CompilerParams(vmem_limit_bytes=VMEM, **kw)


def message_kernel(pos, nrm, area, rad, vis, msg, geom, buf):
    quad = lax.axis_index("quad")
    buf[...] = jnp.zeros_like(buf)
    rows = jnp.zeros((TILES, vis.shape[1]), F32)
    for q in range(vis.shape[0] // TILES):
        part = vis[q * TILES : (q + 1) * TILES, :].astype(F32)
        rows = rows + jnp.where(quad == q, 1.0, 0.0) * part
    for t in range(TILES):
        cols = slice(t * TILE, (t + 1) * TILE)
        buf[16 * t : 16 * t + 3, :] = pos[:, cols].astype(F32)
        buf[16 * t + 3 : 16 * t + 6, :] = nrm[:, cols].astype(F32)
        own = area[:, cols].astype(F32)
        buf[16 * t + 6 : 16 * t + 7, :] = own
        for k in range(vis.shape[1] // TILE):
            buf[16 * t + 8 + k : 16 * t + 9 + k, :] = rows[t : t + 1, k * TILE : (k + 1) * TILE]
        lanes = jnp.broadcast_to(own, (TILE, TILE)).T
        msg[cols, :] = (lanes * rad[cols, :]).astype(BF16)
    packed = buf[...].astype(BF16)
    msg[SUB:, :] = packed
    geom[...] = packed


def make_message(pos, nrm, area, rad, vis):
    return pl.pallas_call(
        message_kernel,
        out_shape=(
            jax.ShapeDtypeStruct((MSG, CASES), BF16),
            jax.ShapeDtypeStruct((GEOM, TILE), BF16),
        ),
        scratch_shapes=[pltpu.VMEM((GEOM, TILE), F32)],
        compiler_params=params(),
    )(pos, nrm, area, rad, vis)


def write_parts(flat, parts):
    parts[...] = jnp.zeros_like(parts)
    parts[:8, :] = flat
    pos = [flat[i : i + 1, :] for i in range(3)]
    nrm = [flat[3 + i : 4 + i, :] for i in range(3)]
    size = pos[0] * pos[0] + pos[1] * pos[1] + pos[2] * pos[2] + flat[6:7, :]
    along = nrm[0] * pos[0] + nrm[1] * pos[1] + nrm[2] * pos[2]
    for first, rest in ((SIZE, size), (ALONG, along)):
        for k in range(3):
            part = rest.astype(BF16).astype(F32)
            rest = rest - part
            parts[first + k : first + k + 1, :] = part
    parts[ONES : ONES + 3, :] = jnp.ones((3, flat.shape[1]), F32)


def rows_kernel(geom, expand, out, seen, flat, parts, wide):
    tiles = geom.shape[0] // 16
    wide[...] = geom[...].astype(F32)
    for r in range(tiles):
        flat[:, r * TILE : (r + 1) * TILE] = wide[16 * r : 16 * r + 8, :]
    for k in range(seen.shape[0]):
        seen[k] = wide[pl.ds(8 + k, tiles, stride=16), :].astype(BF16)
    write_parts(flat[...], parts)
    for r in range(tiles):
        turned = parts[:, r * TILE : (r + 1) * TILE].T.astype(BF16)
        for q in range(3):
            left = jnp.dot(turned, expand[q], preferred_element_type=F32)
            if q == 1:
                lane = lax.broadcasted_iota(jnp.int32, left.shape, 1)
                left = jnp.where(lane == MASK + r, 1.0, left)
            out[q, r * TILE : (r + 1) * TILE, :] = left.astype(BF16)


def make_rows(geom, expand, tile_blocks):
    tiles = geom.shape[0] // 16
    return pl.pallas_call(
        rows_kernel,
        out_shape=(
            jax.ShapeDtypeStruct((3, tiles * TILE, SLOTS), BF16),
            jax.ShapeDtypeStruct((tile_blocks, tiles, TILE), BF16),
        ),
        scratch_shapes=[
            pltpu.VMEM((8, tiles * TILE), F32),
            pltpu.VMEM((128, tiles * TILE), F32),
            pltpu.VMEM(geom.shape, F32),
        ],
        compiler_params=params(),
    )(geom, expand)


def place():
    blk, quad = lax.axis_index("blk"), lax.axis_index("quad")
    return quad % 4, (quad // 4) * 2 + (blk // 2) % 2, blk // 4, blk % 2


def cols_kernel(dys, *refs):
    groups = refs[: len(dys)]
    seen, out, weights, flat, parts = refs[len(dys) :]
    x, y, z, core = place()
    tiles = len(dys) * 4 * TILES
    column = lax.broadcasted_iota(jnp.int32, (TILE, TILE), 1)
    shard = column // TILES
    there_y = (y + dys[0]) % 4
    for n, dy in enumerate(dys[1:], 1):
        there_y = jnp.where(shard // 4 == n, (y + dy) % 4, there_y)
    there_x = (x + shard) % 4
    blk = (z * 2 + there_y % 2) * 2 + core
    tile = blk * 32 + ((there_y // 2) * 4 + there_x) * TILES + column % TILES
    tile = jnp.where(column < tiles, tile, -1)
    index = lax.broadcasted_iota(jnp.int32, (TILE, TILE), 0)
    pair = jnp.zeros((seen.shape[1], TILE), F32)
    for k in range(seen.shape[0]):
        pick = jnp.where(index + k * TILE == tile, 1.0, 0.0).astype(BF16)
        pair = pair + jnp.dot(seen[k], pick, preferred_element_type=F32)
    for n, group in enumerate(groups):
        for s in range(4):
            weights[(4 * n + s) * SUB : (4 * n + s + 1) * SUB, :] = group[s * MSG : s * MSG + SUB, :]
            for t in range(TILES):
                row = s * MSG + SUB + 16 * t
                j = (4 * n + s) * TILES + t
                flat[:, j * TILE : (j + 1) * TILE] = group[row : row + 16, :].astype(F32)[:8, :]
    write_parts(flat[...], parts)
    pair = pair.astype(BF16)
    for s in range(tiles // 4):
        span = slice(s * SUB, (s + 1) * SUB)
        j = lax.broadcasted_iota(jnp.int32, (TILE, SUB), 0)
        c = lax.broadcasted_iota(jnp.int32, (TILE, SUB), 1)
        spread = jnp.where(j == s * TILES + c // TILE, 1.0, 0.0).astype(BF16)
        open_ = jnp.dot(pair, spread, preferred_element_type=F32)
        out[:MASK, span] = parts[:, span].astype(BF16)
        out[MASK:, span] = ((open_ - 1.0) * 64.0).astype(BF16)


def make_cols(groups, dys, seen):
    cols = len(dys) * 4 * SUB
    return pl.pallas_call(
        functools.partial(cols_kernel, dys),
        out_shape=(
            jax.ShapeDtypeStruct((SLOTS, cols), BF16),
            jax.ShapeDtypeStruct((cols, CASES), BF16),
        ),
        scratch_shapes=[pltpu.VMEM((8, cols), F32), pltpu.VMEM((PARTS, cols), F32)],
        compiler_params=params(),
    )(*groups, seen)


def sweep_kernel(first, has_total, *refs):
    left, right, weights = refs[:3]
    total = refs[3] if has_total else None
    out, terms = refs[-2:]
    chunks = right.shape[1] // CHUNK
    steps = out.shape[0] // ROWS * chunks
    out[...] = total[...] if has_total else jnp.zeros_like(out)

    def generate(step, slot):
        base = step // chunks * ROWS
        col = step % chunks * CHUNK
        for c0 in range(0, CHUNK, 256):
            there = right[:, pl.ds(pl.multiple_of(col + c0, 256), 256)]
            for r0 in range(0, ROWS, 128):
                here = pl.ds(pl.multiple_of(first + base + r0, 128), 128)
                den, face_row, face_col = (
                    jnp.dot(left[q, here, :], there, preferred_element_type=F32) for q in range(3)
                )
                inv = pltpu.reciprocal(den, approx=True)
                term = (jnp.maximum(face_row, 0.0) * inv) * (jnp.maximum(face_col, 0.0) * inv)
                terms[slot, r0 : r0 + 128, c0 : c0 + 256] = term.astype(BF16)

    def gather(step, slot):
        base = pl.multiple_of(step // chunks * ROWS, ROWS)
        col = pl.multiple_of(step % chunks * CHUNK, CHUNK)
        out[pl.ds(base, ROWS), :] += jnp.dot(
            terms[slot], weights[pl.ds(col, CHUNK), :], preferred_element_type=F32
        )

    generate(0, 0)

    def body(i, carry):
        step = i * 2
        gather(step, 0)
        generate(step + 1, 1)
        gather(step + 1, 1)
        generate(jnp.minimum(step + 2, steps - 1), 0)
        return carry

    lax.fori_loop(0, steps // 2, body, 0)


def sweep(left, right, weights, total, first, rows):
    has_total = total is not None
    cols = right.shape[1]
    return pl.pallas_call(
        functools.partial(sweep_kernel, first, has_total),
        out_shape=jax.ShapeDtypeStruct((rows, CASES), F32),
        scratch_shapes=[pltpu.VMEM((2, ROWS, CHUNK), BF16)],
        compiler_params=params(),
        cost_estimate=pl.CostEstimate(
            flops=2 * rows * cols * 1024, bytes_accessed=1 << 20, transcendentals=rows * cols
        ),
    )(left, right, weights, *([total] if has_total else []))


def linear(x, y, z, core):
    return ((z * 2 + y % 2) * 2 + core) * 8 + (y // 2) * 4 + x


def shift(value, dx=0, dy=0, dz=0, dc=0):
    pairs = [
        (linear(x, y, z, c), linear((x + dx) % 4, (y + dy) % 4, (z + dz) % 4, (c + dc) % 2))
        for x in range(4)
        for y in range(4)
        for z in range(4)
        for c in range(2)
    ]
    return lax.ppermute(value, AXES, pairs)


def shards(positions, normals, patch_area, reflect, emission, radiosity, visible):
    lhs = jnp.asarray(expansions(), BF16)
    message, geom = make_message(positions, normals, patch_area[None, :], radiosity, visible)
    line = jnp.stack([geom] + [shift(geom, dz=-d) for d in (1, 2, 3)])
    other = shift(line, dc=1)
    row_geom = jnp.stack([line, other], 1).reshape(8 * GEOM, TILE)
    near = jnp.concatenate([message] + [shift(message, dx=-d) for d in (1, 2, 3)])
    far = {d: shift(near, dy=-d) for d in (1, 3, 2)}
    left, seen = make_rows(row_geom, lhs, visible.shape[1] // TILE)
    right, weights = make_cols([near], [0], seen)
    total = sweep(left, right, weights, None, 0, 8 * SUB)
    right, weights = make_cols([far[1]], [1], seen)
    total = sweep(left, right, weights, total, 0, 8 * SUB)
    right, weights = make_cols([far[3], far[2]], [3, 2], seen)
    sums = []
    for d in (2, 1, 3, 0):
        part = sweep(left, right, weights, total[d * 2 * SUB : (d + 1) * 2 * SUB], d * 2 * SUB, 2 * SUB)
        part = part[:SUB] + shift(part[SUB:], dc=1)
        sums.append(shift(part, dz=d) if d else part)
    irradiation = (sums[0] + sums[1]) + (sums[2] + sums[3])
    return emission + (reflect * (1.0 / math.pi))[:, None] * irradiation


def solution(mesh):
    in_specs = (
        P(None, AXES),
        P(None, AXES),
        P(AXES),
        P(AXES),
        P(AXES, None),
        P(AXES, None),
        P("blk", None),
    )
    return jax.shard_map(
        shards, mesh=mesh, in_specs=in_specs, out_specs=P(AXES, None), check_vma=False
    )
```

```python
import functools
import math

import numpy as np

import jax
import jax.numpy as jnp
from jax import lax
from jax.experimental import pallas as pl
from jax.experimental.pallas import tpu as pltpu
from jax.sharding import PartitionSpec as P

BF16, F32 = jnp.bfloat16, jnp.float32
AXES = ("blk", "quad")
SUB = 512
TILE = 128
CASES = 128
TILES = SUB // TILE
GEOM = 16 * TILES
MSG = SUB + GEOM
SLOTS = 64
MASK = 32
CHUNK = 512
ROWS = 1024
VMEM = 56 << 20

SIZE, ALONG, ONES = 8, 11, 14
PARTS = 32


def expansions():
    den, face_row, face_col = (np.zeros((128, SLOTS), np.float32) for _ in range(3))
    for i in range(3):
        den[i, i] = -2
        den[ONES, SIZE + i] = 1
        den[SIZE + i, ONES + i] = 1
        face_row[3 + i, i] = 1
        face_row[ALONG + i, ONES + i] = -1
        face_col[i, 3 + i] = 1
        face_col[ONES, ALONG + i] = -1
    return np.stack([den, face_row, face_col])


def params(**kw):
    return pltpu.CompilerParams(vmem_limit_bytes=VMEM, **kw)


def message_kernel(pos, nrm, area, rad, vis, msg, geom, buf):
    quad = lax.axis_index("quad")
    buf[...] = jnp.zeros_like(buf)
    rows = jnp.zeros((TILES, vis.shape[1]), F32)
    for q in range(vis.shape[0] // TILES):
        part = vis[q * TILES : (q + 1) * TILES, :].astype(F32)
        rows = rows + jnp.where(quad == q, 1.0, 0.0) * part
    for t in range(TILES):
        cols = slice(t * TILE, (t + 1) * TILE)
        buf[16 * t : 16 * t + 3, :] = pos[:, cols].astype(F32)
        buf[16 * t + 3 : 16 * t + 6, :] = nrm[:, cols].astype(F32)
        own = area[:, cols].astype(F32)
        buf[16 * t + 6 : 16 * t + 7, :] = own
        for k in range(vis.shape[1] // TILE):
            buf[16 * t + 8 + k : 16 * t + 9 + k, :] = rows[t : t + 1, k * TILE : (k + 1) * TILE]
        lanes = jnp.broadcast_to(own, (TILE, TILE)).T
        msg[cols, :] = (lanes * rad[cols, :]).astype(BF16)
    packed = buf[...].astype(BF16)
    msg[SUB:, :] = packed
    geom[...] = packed


def make_message(pos, nrm, area, rad, vis):
    return pl.pallas_call(
        message_kernel,
        out_shape=(
            jax.ShapeDtypeStruct((MSG, CASES), BF16),
            jax.ShapeDtypeStruct((GEOM, TILE), BF16),
        ),
        scratch_shapes=[pltpu.VMEM((GEOM, TILE), F32)],
        compiler_params=params(),
    )(pos, nrm, area, rad, vis)


def write_parts(flat, parts):
    parts[...] = jnp.zeros_like(parts)
    parts[:8, :] = flat
    pos = [flat[i : i + 1, :] for i in range(3)]
    nrm = [flat[3 + i : 4 + i, :] for i in range(3)]
    size = pos[0] * pos[0] + pos[1] * pos[1] + pos[2] * pos[2] + flat[6:7, :]
    along = nrm[0] * pos[0] + nrm[1] * pos[1] + nrm[2] * pos[2]
    for first, rest in ((SIZE, size), (ALONG, along)):
        for k in range(3):
            part = rest.astype(BF16).astype(F32)
            rest = rest - part
            parts[first + k : first + k + 1, :] = part
    parts[ONES : ONES + 3, :] = jnp.ones((3, flat.shape[1]), F32)


def rows_kernel(geom, expand, out, seen, flat, parts, wide):
    tiles = geom.shape[0] // 16
    wide[...] = geom[...].astype(F32)
    for r in range(tiles):
        flat[:, r * TILE : (r + 1) * TILE] = wide[16 * r : 16 * r + 8, :]
    for k in range(seen.shape[0]):
        seen[k] = wide[pl.ds(8 + k, tiles, stride=16), :].astype(BF16)
    write_parts(flat[...], parts)
    for r in range(tiles):
        turned = parts[:, r * TILE : (r + 1) * TILE].T.astype(BF16)
        for q in range(3):
            left = jnp.dot(turned, expand[q], preferred_element_type=F32)
            if q == 1:
                lane = lax.broadcasted_iota(jnp.int32, left.shape, 1)
                left = jnp.where(lane == MASK + r, 1.0, left)
            out[q, r * TILE : (r + 1) * TILE, :] = left.astype(BF16)


def make_rows(geom, expand, tile_blocks):
    tiles = geom.shape[0] // 16
    return pl.pallas_call(
        rows_kernel,
        out_shape=(
            jax.ShapeDtypeStruct((3, tiles * TILE, SLOTS), BF16),
            jax.ShapeDtypeStruct((tile_blocks, tiles, TILE), BF16),
        ),
        scratch_shapes=[
            pltpu.VMEM((8, tiles * TILE), F32),
            pltpu.VMEM((128, tiles * TILE), F32),
            pltpu.VMEM(geom.shape, F32),
        ],
        compiler_params=params(),
    )(geom, expand)


def place():
    blk, quad = lax.axis_index("blk"), lax.axis_index("quad")
    return quad % 4, (quad // 4) * 2 + (blk // 2) % 2, blk // 4, blk % 2


def cols_kernel(dys, *refs):
    groups = refs[: len(dys)]
    seen, out, weights, flat, parts = refs[len(dys) :]
    x, y, z, core = place()
    tiles = len(dys) * 4 * TILES
    column = lax.broadcasted_iota(jnp.int32, (TILE, TILE), 1)
    shard = column // TILES
    there_y = (y + dys[0]) % 4
    for n, dy in enumerate(dys[1:], 1):
        there_y = jnp.where(shard // 4 == n, (y + dy) % 4, there_y)
    there_x = (x + shard) % 4
    blk = (z * 2 + there_y % 2) * 2 + core
    tile = blk * 32 + ((there_y // 2) * 4 + there_x) * TILES + column % TILES
    tile = jnp.where(column < tiles, tile, -1)
    index = lax.broadcasted_iota(jnp.int32, (TILE, TILE), 0)
    pair = jnp.zeros((seen.shape[1], TILE), F32)
    for k in range(seen.shape[0]):
        pick = jnp.where(index + k * TILE == tile, 1.0, 0.0).astype(BF16)
        pair = pair + jnp.dot(seen[k], pick, preferred_element_type=F32)
    for n, group in enumerate(groups):
        for s in range(4):
            weights[(4 * n + s) * SUB : (4 * n + s + 1) * SUB, :] = group[s * MSG : s * MSG + SUB, :]
            for t in range(TILES):
                row = s * MSG + SUB + 16 * t
                j = (4 * n + s) * TILES + t
                flat[:, j * TILE : (j + 1) * TILE] = group[row : row + 16, :].astype(F32)[:8, :]
    write_parts(flat[...], parts)
    pair = pair.astype(BF16)
    for s in range(tiles // 4):
        span = slice(s * SUB, (s + 1) * SUB)
        j = lax.broadcasted_iota(jnp.int32, (TILE, SUB), 0)
        c = lax.broadcasted_iota(jnp.int32, (TILE, SUB), 1)
        spread = jnp.where(j == s * TILES + c // TILE, 1.0, 0.0).astype(BF16)
        open_ = jnp.dot(pair, spread, preferred_element_type=F32)
        out[:MASK, span] = parts[:, span].astype(BF16)
        out[MASK:, span] = ((open_ - 1.0) * 64.0).astype(BF16)


def make_cols(groups, dys, seen):
    cols = len(dys) * 4 * SUB
    return pl.pallas_call(
        functools.partial(cols_kernel, dys),
        out_shape=(
            jax.ShapeDtypeStruct((SLOTS, cols), BF16),
            jax.ShapeDtypeStruct((cols, CASES), BF16),
        ),
        scratch_shapes=[pltpu.VMEM((8, cols), F32), pltpu.VMEM((PARTS, cols), F32)],
        compiler_params=params(),
    )(*groups, seen)


def sweep_kernel(first, has_total, *refs):
    left, right, weights = refs[:3]
    out, terms = refs[-2:]
    chunks = right.shape[1] // CHUNK
    count = out.shape[0]
    steps = count // ROWS * chunks
    out[...] = refs[3][first : first + count, :] if has_total else jnp.zeros_like(out)

    def generate(step, slot):
        base = step // chunks * ROWS
        col = step % chunks * CHUNK
        for c0 in range(0, CHUNK, 256):
            cols = pl.ds(pl.multiple_of(col + c0, 256), 256)
            there = right[:, cols]
            for r0 in range(0, ROWS, 128):
                here = pl.ds(pl.multiple_of(first + base + r0, 128), 128)
                den, face_row, face_col = (
                    jnp.dot(left[q, here, :], there, preferred_element_type=F32) for q in range(3)
                )
                inv = pltpu.reciprocal(den, approx=True)
                term = (jnp.maximum(face_row, 0.0) * inv) * (jnp.maximum(face_col, 0.0) * inv)
                terms[slot, r0 : r0 + 128, c0 : c0 + 256] = term.astype(BF16)

    def gather(step, slot):
        base = pl.multiple_of(step // chunks * ROWS, ROWS)
        col = pl.multiple_of(step % chunks * CHUNK, CHUNK)
        out[pl.ds(base, ROWS), :] += jnp.dot(
            terms[slot], weights[pl.ds(col, CHUNK), :], preferred_element_type=F32
        )

    generate(0, 0)

    def body(i, carry):
        step = i * 2
        gather(step, 0)
        generate(step + 1, 1)
        gather(step + 1, 1)
        generate(step + 2, 0)
        return carry

    lax.fori_loop(0, steps // 2 - 1, body, 0)
    gather(steps - 2, 0)
    generate(steps - 1, 1)
    gather(steps - 1, 1)


def sweep(left, cols, total, first, count):
    has_total = total is not None
    width = cols[0].shape[1]
    return pl.pallas_call(
        functools.partial(sweep_kernel, first, has_total),
        out_shape=jax.ShapeDtypeStruct((count, CASES), F32),
        scratch_shapes=[pltpu.VMEM((2, ROWS, CHUNK), BF16)],
        compiler_params=params(),
        cost_estimate=pl.CostEstimate(
            flops=2 * count * width * 1536, bytes_accessed=1 << 20, transcendentals=count * width
        ),
    )(left, *cols, *([total] if has_total else []))


def linear(x, y, z, core):
    return ((z * 2 + y % 2) * 2 + core) * 8 + (y // 2) * 4 + x


def shift(value, dx=0, dy=0, dz=0, dc=0):
    pairs = [
        (linear(x, y, z, c), linear((x + dx) % 4, (y + dy) % 4, (z + dz) % 4, (c + dc) % 2))
        for x in range(4)
        for y in range(4)
        for z in range(4)
        for c in range(2)
    ]
    return lax.ppermute(value, AXES, pairs)


def shards(positions, normals, patch_area, reflect, emission, radiosity, visible):
    lhs = jnp.asarray(expansions(), BF16)
    message, geom = make_message(positions, normals, patch_area[None, :], radiosity, visible)
    line = jnp.stack([geom] + [shift(geom, dz=-d) for d in (1, 2, 3)])
    other = shift(line, dc=1)
    row_geom = jnp.stack([line, other], 1).reshape(8 * GEOM, TILE)
    near = jnp.concatenate([message] + [shift(message, dx=-d) for d in (1, 2, 3)])
    far = {d: shift(near, dy=-d) for d in (1, 3, 2)}
    left, seen = make_rows(row_geom, lhs, visible.shape[1] // TILE)
    total = sweep(left, make_cols([near], [0], seen), None, 0, 8 * SUB)
    total = sweep(left, make_cols([far[1]], [1], seen), total, 0, 8 * SUB)
    cols = make_cols([far[3], far[2]], [3, 2], seen)
    part = sweep(left, cols, total, 2 * SUB, 6 * SUB).reshape(3, 2, SUB, CASES)
    away = part[:, 0] + shift(part[:, 1], dc=1)
    away, cols = lax.optimization_barrier((away, cols))
    sent = [shift(away[d - 1], dz=d) for d in (2, 1, 3)]
    part = sweep(left, cols, total, 0, 2 * SUB)
    own = part[:SUB] + shift(part[SUB:], dc=1)
    irradiation = own + (sent[0] + sent[1] + sent[2])
    return emission + (reflect * (1.0 / math.pi))[:, None] * irradiation


def solution(mesh):
    in_specs = (
        P(None, AXES),
        P(None, AXES),
        P(AXES),
        P(AXES),
        P(AXES, None),
        P(AXES, None),
        P("blk", None),
    )
    return jax.shard_map(
        shards, mesh=mesh, in_specs=in_specs, out_specs=P(AXES, None), check_vma=False
    )
```

```python
import functools
import math

import numpy as np

import jax
import jax.numpy as jnp
from jax import lax
from jax.experimental import pallas as pl
from jax.experimental.pallas import tpu as pltpu
from jax.sharding import PartitionSpec as P

BF16, F32 = jnp.bfloat16, jnp.float32
AXES = ("blk", "quad")
SUB = 512
TILE = 128
CASES = 128
TILES = SUB // TILE
GEOM = 16 * TILES
MSG = SUB + GEOM
SLOTS = 64
MASK = 32
CHUNK = 1024
ROWS = 1024
VMEM = 56 << 20

SIZE, ALONG, ONES = 8, 11, 14
PARTS = 32


def expansions():
    den, face_row, face_col = (np.zeros((128, SLOTS), np.float32) for _ in range(3))
    for i in range(3):
        den[i, i] = -2
        den[ONES, SIZE + i] = 1
        den[SIZE + i, ONES + i] = 1
        face_row[3 + i, i] = 1
        face_row[ALONG + i, ONES + i] = -1
        face_col[i, 3 + i] = 1
        face_col[ONES, ALONG + i] = -1
    return np.stack([den, face_row, face_col])


def params(**kw):
    return pltpu.CompilerParams(vmem_limit_bytes=VMEM, **kw)


def message_kernel(pos, nrm, area, rad, vis, msg, geom, buf):
    quad = lax.axis_index("quad")
    buf[...] = jnp.zeros_like(buf)
    rows = jnp.zeros((TILES, vis.shape[1]), F32)
    for q in range(vis.shape[0] // TILES):
        part = vis[q * TILES : (q + 1) * TILES, :].astype(F32)
        rows = rows + jnp.where(quad == q, 1.0, 0.0) * part
    for t in range(TILES):
        cols = slice(t * TILE, (t + 1) * TILE)
        buf[16 * t : 16 * t + 3, :] = pos[:, cols].astype(F32)
        buf[16 * t + 3 : 16 * t + 6, :] = nrm[:, cols].astype(F32)
        own = area[:, cols].astype(F32)
        buf[16 * t + 6 : 16 * t + 7, :] = own
        for k in range(vis.shape[1] // TILE):
            buf[16 * t + 8 + k : 16 * t + 9 + k, :] = rows[t : t + 1, k * TILE : (k + 1) * TILE]
        lanes = jnp.broadcast_to(own, (TILE, TILE)).T
        msg[cols, :] = (lanes * rad[cols, :]).astype(BF16)
    packed = buf[...].astype(BF16)
    msg[SUB:, :] = packed
    geom[...] = packed


def make_message(pos, nrm, area, rad, vis):
    return pl.pallas_call(
        message_kernel,
        out_shape=(
            jax.ShapeDtypeStruct((MSG, CASES), BF16),
            jax.ShapeDtypeStruct((GEOM, TILE), BF16),
        ),
        scratch_shapes=[pltpu.VMEM((GEOM, TILE), F32)],
        compiler_params=params(),
    )(pos, nrm, area, rad, vis)


def write_parts(flat, parts):
    parts[...] = jnp.zeros_like(parts)
    parts[:8, :] = flat
    pos = [flat[i : i + 1, :] for i in range(3)]
    nrm = [flat[3 + i : 4 + i, :] for i in range(3)]
    size = pos[0] * pos[0] + pos[1] * pos[1] + pos[2] * pos[2] + flat[6:7, :]
    along = nrm[0] * pos[0] + nrm[1] * pos[1] + nrm[2] * pos[2]
    for first, rest in ((SIZE, size), (ALONG, along)):
        for k in range(3):
            part = rest.astype(BF16).astype(F32)
            rest = rest - part
            parts[first + k : first + k + 1, :] = part
    parts[ONES : ONES + 3, :] = jnp.ones((3, flat.shape[1]), F32)


def rows_kernel(geom, expand, out, seen, flat, parts, wide):
    tiles = geom.shape[0] // 16
    wide[...] = geom[...].astype(F32)
    for r in range(tiles):
        flat[:, r * TILE : (r + 1) * TILE] = wide[16 * r : 16 * r + 8, :]
    for k in range(seen.shape[0]):
        seen[k] = wide[pl.ds(8 + k, tiles, stride=16), :].astype(BF16)
    write_parts(flat[...], parts)
    for r in range(tiles):
        turned = parts[:, r * TILE : (r + 1) * TILE].T.astype(BF16)
        for q in range(3):
            left = jnp.dot(turned, expand[q], preferred_element_type=F32)
            if q == 1:
                lane = lax.broadcasted_iota(jnp.int32, left.shape, 1)
                left = jnp.where(lane == MASK + r, 1.0, left)
            out[q, r * TILE : (r + 1) * TILE, :] = left.astype(BF16)


def make_rows(geom, expand, tile_blocks):
    tiles = geom.shape[0] // 16
    return pl.pallas_call(
        rows_kernel,
        out_shape=(
            jax.ShapeDtypeStruct((3, tiles * TILE, SLOTS), BF16),
            jax.ShapeDtypeStruct((tile_blocks, tiles, TILE), BF16),
        ),
        scratch_shapes=[
            pltpu.VMEM((8, tiles * TILE), F32),
            pltpu.VMEM((128, tiles * TILE), F32),
            pltpu.VMEM(geom.shape, F32),
        ],
        compiler_params=params(),
    )(geom, expand)


def place():
    blk, quad = lax.axis_index("blk"), lax.axis_index("quad")
    return quad % 4, (quad // 4) * 2 + (blk // 2) % 2, blk // 4, blk % 2


def cols_kernel(dys, *refs):
    groups = refs[: len(dys)]
    seen, out, weights, flat, parts = refs[len(dys) :]
    x, y, z, core = place()
    tiles = len(dys) * 4 * TILES
    column = lax.broadcasted_iota(jnp.int32, (TILE, TILE), 1)
    shard = column // TILES
    there_y = (y + dys[0]) % 4
    for n, dy in enumerate(dys[1:], 1):
        there_y = jnp.where(shard // 4 == n, (y + dy) % 4, there_y)
    there_x = (x + shard) % 4
    blk = (z * 2 + there_y % 2) * 2 + core
    tile = blk * 32 + ((there_y // 2) * 4 + there_x) * TILES + column % TILES
    tile = jnp.where(column < tiles, tile, -1)
    index = lax.broadcasted_iota(jnp.int32, (TILE, TILE), 0)
    pair = jnp.zeros((seen.shape[1], TILE), F32)
    for k in range(seen.shape[0]):
        pick = jnp.where(index + k * TILE == tile, 1.0, 0.0).astype(BF16)
        pair = pair + jnp.dot(seen[k], pick, preferred_element_type=F32)
    for n, group in enumerate(groups):
        for s in range(4):
            weights[(4 * n + s) * SUB : (4 * n + s + 1) * SUB, :] = group[s * MSG : s * MSG + SUB, :]
            for t in range(TILES):
                row = s * MSG + SUB + 16 * t
                j = (4 * n + s) * TILES + t
                flat[:, j * TILE : (j + 1) * TILE] = group[row : row + 16, :].astype(F32)[:8, :]
    write_parts(flat[...], parts)
    pair = pair.astype(BF16)
    for s in range(tiles // 4):
        span = slice(s * SUB, (s + 1) * SUB)
        j = lax.broadcasted_iota(jnp.int32, (TILE, SUB), 0)
        c = lax.broadcasted_iota(jnp.int32, (TILE, SUB), 1)
        spread = jnp.where(j == s * TILES + c // TILE, 1.0, 0.0).astype(BF16)
        open_ = jnp.dot(pair, spread, preferred_element_type=F32)
        out[:MASK, span] = parts[:, span].astype(BF16)
        out[MASK:, span] = ((open_ - 1.0) * 64.0).astype(BF16)


def make_cols(groups, dys, seen):
    cols = len(dys) * 4 * SUB
    return pl.pallas_call(
        functools.partial(cols_kernel, dys),
        out_shape=(
            jax.ShapeDtypeStruct((SLOTS, cols), BF16),
            jax.ShapeDtypeStruct((cols, CASES), BF16),
        ),
        scratch_shapes=[pltpu.VMEM((8, cols), F32), pltpu.VMEM((PARTS, cols), F32)],
        compiler_params=params(),
    )(*groups, seen)


def sweep_kernel(first, has_total, split, *refs):
    left, right, weights = refs[:3]
    if split:
        near, far, terms, out = refs[-4:]
    else:
        out, terms = refs[-2:]
    chunks = right.shape[1] // CHUNK
    count = out.shape[0]
    steps = count // ROWS * chunks
    out[...] = refs[3][first : first + count, :] if has_total else jnp.zeros_like(out)

    def generate(step, slot):
        base = step // chunks * ROWS
        col = step % chunks * CHUNK
        for c0 in range(0, CHUNK, 256):
            cols = pl.ds(pl.multiple_of(col + c0, 256), 256)
            there = right[:, cols]
            for r0 in range(0, ROWS, 128):
                here = pl.ds(pl.multiple_of(first + base + r0, 128), 128)
                den, face_row, face_col = (
                    jnp.dot(left[q, here, :], there, preferred_element_type=F32) for q in range(3)
                )
                inv = pltpu.reciprocal(den, approx=True)
                term = (jnp.maximum(face_row, 0.0) * inv) * (jnp.maximum(face_col, 0.0) * inv)
                terms[slot, r0 : r0 + 128, c0 : c0 + 256] = term.astype(BF16)

    def gather(step, slot):
        base = pl.multiple_of(step // chunks * ROWS, ROWS)
        col = pl.multiple_of(step % chunks * CHUNK, CHUNK)
        out[pl.ds(base, ROWS), :] += jnp.dot(
            terms[slot], weights[pl.ds(col, CHUNK), :], preferred_element_type=F32
        )

    generate(0, 0)

    def body(i, carry):
        step = i * 2
        gather(step, 0)
        generate(step + 1, 1)
        gather(step + 1, 1)
        generate(step + 2, 0)
        return carry

    lax.fori_loop(0, steps // 2 - 1, body, 0)
    gather(steps - 2, 0)
    generate(steps - 1, 1)
    gather(steps - 1, 1)
    if split:
        for n in range(count // (2 * SUB)):
            here = slice(n * SUB, (n + 1) * SUB)
            near[here, :] = out[2 * n * SUB : (2 * n + 1) * SUB, :]
            far[here, :] = out[(2 * n + 1) * SUB : (2 * n + 2) * SUB, :]


def sweep(left, cols, total, first, count, split=False):
    has_total = total is not None
    width = cols[0].shape[1]
    shape = jax.ShapeDtypeStruct((count, CASES), F32)
    half = jax.ShapeDtypeStruct((count // 2, CASES), F32)
    return pl.pallas_call(
        functools.partial(sweep_kernel, first, has_total, split),
        out_shape=(half, half) if split else shape,
        scratch_shapes=[pltpu.VMEM((2, ROWS, CHUNK), BF16)]
        + ([pltpu.VMEM((count, CASES), F32)] if split else []),
        compiler_params=params(),
        cost_estimate=pl.CostEstimate(
            flops=2 * count * width * 1536, bytes_accessed=1 << 20, transcendentals=count * width
        ),
    )(left, *cols, *([total] if has_total else []))


def linear(x, y, z, core):
    return ((z * 2 + y % 2) * 2 + core) * 8 + (y // 2) * 4 + x


def shift(value, dx=0, dy=0, dz=0, dc=0):
    pairs = [
        (linear(x, y, z, c), linear((x + dx) % 4, (y + dy) % 4, (z + dz) % 4, (c + dc) % 2))
        for x in range(4)
        for y in range(4)
        for z in range(4)
        for c in range(2)
    ]
    return lax.ppermute(value, AXES, pairs)


def shards(positions, normals, patch_area, reflect, emission, radiosity, visible):
    lhs = jnp.asarray(expansions(), BF16)
    message, geom = make_message(positions, normals, patch_area[None, :], radiosity, visible)
    line = jnp.stack([geom] + [shift(geom, dz=-d) for d in (1, 2, 3)])
    other = shift(line, dc=1)
    row_geom = jnp.stack([line, other], 1).reshape(8 * GEOM, TILE)
    near = jnp.concatenate([message] + [shift(message, dx=-d) for d in (1, 2, 3)])
    far = {d: shift(near, dy=-d) for d in (1, 3, 2)}
    left, seen = make_rows(row_geom, lhs, visible.shape[1] // TILE)
    total = sweep(left, make_cols([near], [0], seen), None, 0, 8 * SUB)
    cols = make_cols([far[1], far[3], far[2]], [1, 3, 2], seen)
    mine, others = sweep(left, cols, total, 2 * SUB, 6 * SUB, True)
    away = mine + shift(others, dc=1)
    away, cols = lax.optimization_barrier((away, cols))
    sent = [shift(away[(d - 1) * SUB : d * SUB], dz=d) for d in (2, 1, 3)]
    mine, others = sweep(left, cols, total, 0, 2 * SUB, True)
    own = mine + shift(others, dc=1)
    irradiation = own + (sent[0] + sent[1] + sent[2])
    return emission + (reflect * (1.0 / math.pi))[:, None] * irradiation


def solution(mesh):
    in_specs = (
        P(None, AXES),
        P(None, AXES),
        P(AXES),
        P(AXES),
        P(AXES, None),
        P(AXES, None),
        P("blk", None),
    )
    return jax.shard_map(
        shards, mesh=mesh, in_specs=in_specs, out_specs=P(AXES, None), check_vma=False
    )
```

```python
import functools
import math

import numpy as np

import jax
import jax.numpy as jnp
from jax import lax
from jax.experimental import pallas as pl
from jax.experimental.pallas import tpu as pltpu
from jax.sharding import PartitionSpec as P

BF16, F32 = jnp.bfloat16, jnp.float32
AXES = ("blk", "quad")
SUB = 512
TILE = 128
CASES = 128
TILES = SUB // TILE
GEOM = 16 * TILES
MSG = SUB + GEOM
SLOTS = 64
MASK = 32
CHUNK = 1024
ROWS = 1024
VMEM = 56 << 20

SIZE, ALONG, ONES = 8, 11, 14
PARTS = 32


def expansions():
    den, face_row, face_col = (np.zeros((PARTS, SLOTS), np.float32) for _ in range(3))
    for i in range(3):
        den[i, i] = -2
        den[ONES, SIZE + i] = 1
        den[SIZE + i, ONES + i] = 1
        face_row[3 + i, i] = 1
        face_row[ALONG + i, ONES + i] = -1
        face_col[i, 3 + i] = 1
        face_col[ONES, ALONG + i] = -1
    return np.stack([den, face_row, face_col])


def params(**kw):
    return pltpu.CompilerParams(vmem_limit_bytes=VMEM, **kw)


def message_kernel(pos, nrm, area, rad, vis, msg, geom, buf):
    quad = lax.axis_index("quad")
    buf[...] = jnp.zeros_like(buf)
    rows = jnp.zeros((TILES, vis.shape[1]), F32)
    for q in range(vis.shape[0] // TILES):
        part = vis[q * TILES : (q + 1) * TILES, :].astype(F32)
        rows = rows + jnp.where(quad == q, 1.0, 0.0) * part
    for t in range(TILES):
        cols = slice(t * TILE, (t + 1) * TILE)
        buf[16 * t : 16 * t + 3, :] = pos[:, cols].astype(F32)
        buf[16 * t + 3 : 16 * t + 6, :] = nrm[:, cols].astype(F32)
        own = area[:, cols].astype(F32)
        buf[16 * t + 6 : 16 * t + 7, :] = own
        for k in range(vis.shape[1] // TILE):
            buf[16 * t + 8 + k : 16 * t + 9 + k, :] = rows[t : t + 1, k * TILE : (k + 1) * TILE]
        lanes = jnp.broadcast_to(own, (TILE, TILE)).T
        msg[cols, :] = (lanes * rad[cols, :]).astype(BF16)
    packed = buf[...].astype(BF16)
    msg[SUB:, :] = packed
    geom[...] = packed


def make_message(pos, nrm, area, rad, vis):
    return pl.pallas_call(
        message_kernel,
        out_shape=(
            jax.ShapeDtypeStruct((MSG, CASES), BF16),
            jax.ShapeDtypeStruct((GEOM, TILE), BF16),
        ),
        scratch_shapes=[pltpu.VMEM((GEOM, TILE), F32)],
        compiler_params=params(),
    )(pos, nrm, area, rad, vis)


def write_parts(flat, parts):
    parts[...] = jnp.zeros_like(parts)
    parts[:8, :] = flat
    pos = [flat[i : i + 1, :] for i in range(3)]
    nrm = [flat[3 + i : 4 + i, :] for i in range(3)]
    size = pos[0] * pos[0] + pos[1] * pos[1] + pos[2] * pos[2] + flat[6:7, :]
    along = nrm[0] * pos[0] + nrm[1] * pos[1] + nrm[2] * pos[2]
    for first, rest in ((SIZE, size), (ALONG, along)):
        for k in range(3):
            part = rest.astype(BF16).astype(F32)
            rest = rest - part
            parts[first + k : first + k + 1, :] = part
    parts[ONES : ONES + 3, :] = jnp.ones((3, flat.shape[1]), F32)


def rows_kernel(geom, expand, out, seen, flat, parts, wide):
    tiles = geom.shape[0] // 16
    wide[...] = geom[...].astype(F32)
    for r in range(tiles):
        flat[:, r * TILE : (r + 1) * TILE] = wide[16 * r : 16 * r + 8, :]
    for k in range(seen.shape[0]):
        seen[k] = wide[pl.ds(8 + k, tiles, stride=16), :].astype(BF16)
    write_parts(flat[...], parts)
    for r in range(tiles):
        turned = parts[:, r * TILE : (r + 1) * TILE].T.astype(BF16)
        for q in range(3):
            left = jnp.dot(turned, expand[q], preferred_element_type=F32)
            if q == 1:
                lane = lax.broadcasted_iota(jnp.int32, left.shape, 1)
                left = jnp.where(lane == MASK + r, 1.0, left)
            out[q, r * TILE : (r + 1) * TILE, :] = left.astype(BF16)


def make_rows(geom, expand, tile_blocks):
    tiles = geom.shape[0] // 16
    return pl.pallas_call(
        rows_kernel,
        out_shape=(
            jax.ShapeDtypeStruct((3, tiles * TILE, SLOTS), BF16),
            jax.ShapeDtypeStruct((tile_blocks, tiles, TILE), BF16),
        ),
        scratch_shapes=[
            pltpu.VMEM((8, tiles * TILE), F32),
            pltpu.VMEM((PARTS, tiles * TILE), F32),
            pltpu.VMEM(geom.shape, F32),
        ],
        compiler_params=params(),
    )(geom, expand)


def place():
    blk, quad = lax.axis_index("blk"), lax.axis_index("quad")
    return quad % 4, (quad // 4) * 2 + (blk // 2) % 2, blk // 4, blk % 2


def cols_kernel(dys, *refs):
    groups = refs[: len(dys)]
    seen, out, weights, flat, parts = refs[len(dys) :]
    x, y, z, core = place()
    tiles = len(dys) * 4 * TILES
    column = lax.broadcasted_iota(jnp.int32, (TILE, TILE), 1)
    shard = column // TILES
    there_y = (y + dys[0]) % 4
    for n, dy in enumerate(dys[1:], 1):
        there_y = jnp.where(shard // 4 == n, (y + dy) % 4, there_y)
    there_x = (x + shard) % 4
    blk = (z * 2 + there_y % 2) * 2 + core
    tile = blk * 32 + ((there_y // 2) * 4 + there_x) * TILES + column % TILES
    tile = jnp.where(column < tiles, tile, -1)
    index = lax.broadcasted_iota(jnp.int32, (TILE, TILE), 0)
    pair = jnp.zeros((seen.shape[1], TILE), F32)
    for k in range(seen.shape[0]):
        pick = jnp.where(index + k * TILE == tile, 1.0, 0.0).astype(BF16)
        pair = pair + jnp.dot(seen[k], pick, preferred_element_type=F32)
    for n, group in enumerate(groups):
        for s in range(4):
            weights[(4 * n + s) * SUB : (4 * n + s + 1) * SUB, :] = group[s * MSG : s * MSG + SUB, :]
            for t in range(TILES):
                row = s * MSG + SUB + 16 * t
                j = (4 * n + s) * TILES + t
                flat[:, j * TILE : (j + 1) * TILE] = group[row : row + 16, :].astype(F32)[:8, :]
    write_parts(flat[...], parts)
    pair = pair.astype(BF16)
    for s in range(tiles // 4):
        span = slice(s * SUB, (s + 1) * SUB)
        j = lax.broadcasted_iota(jnp.int32, (TILE, SUB), 0)
        c = lax.broadcasted_iota(jnp.int32, (TILE, SUB), 1)
        spread = jnp.where(j == s * TILES + c // TILE, 1.0, 0.0).astype(BF16)
        open_ = jnp.dot(pair, spread, preferred_element_type=F32)
        out[:MASK, span] = parts[:, span].astype(BF16)
        out[MASK:, span] = ((open_ - 1.0) * 64.0).astype(BF16)


def make_cols(groups, dys, seen):
    cols = len(dys) * 4 * SUB
    return pl.pallas_call(
        functools.partial(cols_kernel, dys),
        out_shape=(
            jax.ShapeDtypeStruct((SLOTS, cols), BF16),
            jax.ShapeDtypeStruct((cols, CASES), BF16),
        ),
        scratch_shapes=[pltpu.VMEM((8, cols), F32), pltpu.VMEM((PARTS, cols), F32)],
        compiler_params=params(),
    )(*groups, seen)


def sweep_kernel(first, has_total, split, *refs):
    left, right, weights = refs[:3]
    if split:
        near, far, terms, out = refs[-4:]
    else:
        out, terms = refs[-2:]
    chunks = right.shape[1] // CHUNK
    count = out.shape[0]
    steps = count // ROWS * chunks
    out[...] = refs[3][first : first + count, :] if has_total else jnp.zeros_like(out)

    def generate(step, slot):
        base = step // chunks * ROWS
        col = step % chunks * CHUNK
        for c0 in range(0, CHUNK, 256):
            cols = pl.ds(pl.multiple_of(col + c0, 256), 256)
            there = right[:, cols]
            for r0 in range(0, ROWS, 128):
                here = pl.ds(pl.multiple_of(first + base + r0, 128), 128)
                den, face_row, face_col = (
                    jnp.dot(left[q, here, :], there, preferred_element_type=F32) for q in range(3)
                )
                inv = pltpu.reciprocal(den, approx=True)
                term = (jnp.maximum(face_row, 0.0) * inv) * (jnp.maximum(face_col, 0.0) * inv)
                terms[slot, r0 : r0 + 128, c0 : c0 + 256] = term.astype(BF16)

    def gather(step, slot):
        base = pl.multiple_of(step // chunks * ROWS, ROWS)
        col = pl.multiple_of(step % chunks * CHUNK, CHUNK)
        out[pl.ds(base, ROWS), :] += jnp.dot(
            terms[slot], weights[pl.ds(col, CHUNK), :], preferred_element_type=F32
        )

    generate(0, 0)

    def body(i, carry):
        step = i * 2
        gather(step, 0)
        generate(step + 1, 1)
        gather(step + 1, 1)
        generate(step + 2, 0)
        return carry

    lax.fori_loop(0, steps // 2 - 1, body, 0)
    gather(steps - 2, 0)
    generate(steps - 1, 1)
    gather(steps - 1, 1)
    if split:
        for n in range(count // (2 * SUB)):
            here = slice(n * SUB, (n + 1) * SUB)
            near[here, :] = out[2 * n * SUB : (2 * n + 1) * SUB, :]
            far[here, :] = out[(2 * n + 1) * SUB : (2 * n + 2) * SUB, :]


def sweep(left, cols, total, first, count, split=False):
    has_total = total is not None
    width = cols[0].shape[1]
    shape = jax.ShapeDtypeStruct((count, CASES), F32)
    half = jax.ShapeDtypeStruct((count // 2, CASES), F32)
    return pl.pallas_call(
        functools.partial(sweep_kernel, first, has_total, split),
        out_shape=(half, half) if split else shape,
        scratch_shapes=[pltpu.VMEM((2, ROWS, CHUNK), BF16)]
        + ([pltpu.VMEM((count, CASES), F32)] if split else []),
        compiler_params=params(),
        cost_estimate=pl.CostEstimate(
            flops=2 * count * width * 1536, bytes_accessed=1 << 20, transcendentals=count * width
        ),
    )(left, *cols, *([total] if has_total else []))


def linear(x, y, z, core):
    return ((z * 2 + y % 2) * 2 + core) * 8 + (y // 2) * 4 + x


def shift(value, dx=0, dy=0, dz=0, dc=0):
    pairs = [
        (linear(x, y, z, c), linear((x + dx) % 4, (y + dy) % 4, (z + dz) % 4, (c + dc) % 2))
        for x in range(4)
        for y in range(4)
        for z in range(4)
        for c in range(2)
    ]
    return lax.ppermute(value, AXES, pairs)


def shards(positions, normals, patch_area, reflect, emission, radiosity, visible):
    lhs = jnp.asarray(expansions(), BF16)
    message, geom = make_message(positions, normals, patch_area[None, :], radiosity, visible)
    line = jnp.stack([geom] + [shift(geom, dz=-d) for d in (1, 2, 3)])
    other = shift(line, dc=1)
    row_geom = jnp.stack([line, other], 1).reshape(8 * GEOM, TILE)
    near = jnp.concatenate([message] + [shift(message, dx=-d) for d in (1, 2, 3)])
    far = {d: shift(near, dy=-d) for d in (1, 3, 2)}
    left, seen = make_rows(row_geom, lhs, visible.shape[1] // TILE)
    total = sweep(left, make_cols([near], [0], seen), None, 0, 8 * SUB)
    cols = make_cols([far[1], far[3], far[2]], [1, 3, 2], seen)
    mine, others = sweep(left, cols, total, 2 * SUB, 6 * SUB, True)
    away = mine + shift(others, dc=1)
    away, cols = lax.optimization_barrier((away, cols))
    sent = [shift(away[(d - 1) * SUB : d * SUB], dz=d) for d in (2, 1, 3)]
    mine, others = sweep(left, cols, total, 0, 2 * SUB, True)
    own = mine + shift(others, dc=1)
    irradiation = own + (sent[0] + sent[1] + sent[2])
    return emission + (reflect * (1.0 / math.pi))[:, None] * irradiation


def solution(mesh):
    in_specs = (
        P(None, AXES),
        P(None, AXES),
        P(AXES),
        P(AXES),
        P(AXES, None),
        P(AXES, None),
        P("blk", None),
    )
    return jax.shard_map(
        shards, mesh=mesh, in_specs=in_specs, out_specs=P(AXES, None), check_vma=False
    )
```
